32 devices in a mesh: groups: 2 (over x), mp: 8 (over z, y), dp: 2 (over core).
Axes of the slice: x: 2, y: 2, z: 4, core: 2. Of those that a mesh axis runs over, the one named last changes fastest.
Arguments:
- activations: bfloat16 [2048, 8192], P(('groups', 'dp'), 'mp'), parts along dimension 0, may hold values from -6 to 6
- cotangent: bfloat16 [2048, 14336], P(('groups', 'dp'), 'mp'), parts along dimension 0, may hold values from -6 to 6
- frozen_weight: bfloat16 [8192, 14336], P(None, 'mp'), may hold values from -0.09375 to 0.09375
- adapter_down: bfloat16 [8192, 64], P('mp'), may hold values from -0.0625 to 0.0625
- adapter_up: bfloat16 [64, 14336], P(None, 'mp'), may hold values from -0.75 to 0.75
- sparse_values: bfloat16 [64, 8, 128, 128], P('mp'), may hold values from -0.5 to 0.5
- block_cols: int32 [64, 8], replicated, may hold values from 0 to 111, as said below
- block_count: int32 [64], replicated, may hold values from 0 to 2, as said below
Outputs:
- input_grad: bfloat16 [2048, 8192], P(('groups', 'dp'), 'mp'), parts along dimension 0
- down_grad: float32 [16384, 64], P(('groups', 'mp')), parts along dimension 0
- up_grad: float32 [128, 14336], P('groups', 'mp'), parts along dimension 0
- block_grads: float32 [128, 8, 128, 128], P(('groups', 'mp'), 'dp'), parts along dimension 0
The draws below stay inside these ranges and needn't reach their ends.
There are 2 independent parts, one for each index of `groups`. The reference program is written for one: setup_inputs(seed, part) draws one part's arguments, and reference() takes and returns one part's arrays. A program takes and returns all parts, laid end to end along the dimension named above; an argument that names none is the same for every part. Nothing has to cross between parts.
Inputs may be any that keep to these rules, and one draw needn't show every extreme that they name: `block_cols`: the first block_count[r] entries of block row r are distinct and increasing; the others are 0. Cut the block rows into aligned runs of 8 and the block columns into aligned runs of 14: no run of rows has more than 2 support blocks in one run of columns, and in every run of rows some run of columns has exactly 2. `block_count`: some block row has exactly 2 support blocks.
All inputs are finite; a program needn't handle non-finite values.
Results may differ from the reference program's by a relative error of at most 0.015.
Values may be sent and summed in bfloat16 or wider, within the bound.
A program may use at most 128 MiB of HBM per device.

```python
import jax
import jax.numpy as jnp
from jax import lax

D = 8192
FW = 14336
R = 64
BLK = 128
MAXR = 8
TOKENS = 1024
NBR = 64
NBC = 112
N_MP = 8


def support_tables(key):
    owners = N_MP
    per_owner = D // (BLK * N_MP)
    per_holder = FW // (BLK * N_MP)
    period = per_owner // 2
    keys = jax.random.split(key, 6)
    shift_owner = jax.random.randint(keys[0], (owners,), 0, period, dtype=jnp.int32)
    local_rows = jnp.arange(per_owner, dtype=jnp.int32)
    holders = jnp.arange(owners, dtype=jnp.int32)
    owner_ids = jnp.arange(owners, dtype=jnp.int32)
    eligible = (holders[None, None, :] + local_rows[None, :, None] + shift_owner[:, None, None]) % period == 0
    coin = jax.random.randint(keys[1], (owners, per_owner, owners), 0, 100, dtype=jnp.int32) < 35
    forced_holder = jax.random.randint(keys[2], (owners,), 0, owners, dtype=jnp.int32)
    busy_owner = jax.random.randint(keys[3], (), 0, owners, dtype=jnp.int32)
    busy_row = jax.random.randint(keys[4], (), 0, per_owner, dtype=jnp.int32)
    forced = (holders[None, None, :] == forced_holder[:, None, None]) | (owner_ids[:, None, None] == busy_owner) & (local_rows[None, :, None] == busy_row)
    active = eligible & (coin | forced)
    within = jax.random.randint(keys[5], (owners, per_owner, owners), 0, per_holder, dtype=jnp.int32)
    columns = holders[None, None, :] * per_holder + within
    active_int = active.astype(jnp.int32)
    position = jnp.cumsum(active_int, axis=2) - 1
    slot_ids = jnp.arange(MAXR, dtype=jnp.int32)
    hits = active[:, :, :, None] & (position[:, :, :, None] == slot_ids[None, None, None, :])
    table = jnp.sum(jnp.where(hits, columns[:, :, :, None], 0), axis=2).astype(jnp.int32)
    counts = jnp.sum(active_int, axis=2).astype(jnp.int32)
    return (table.reshape(NBR, MAXR), counts.reshape(NBR))


def draw_block_cols(key, part):
    tables = support_tables(key)
    return tables[0]


def draw_block_count(key, part):
    tables = support_tables(key)
    return tables[1]


def strengthened(drawn, rng, source, target, blocks, factor):
    owner, partner = [(jnp.arange(drawn.shape[dim]) // (drawn.shape[dim] // blocks)).reshape([-1 if axis == dim else 1 for axis in range(drawn.ndim)]) for dim in (source, target)]
    chosen = jax.random.permutation(rng, blocks)[partner]
    strong = (owner == chosen) | (owner == (partner + blocks // 2) % blocks)
    return jnp.where(strong, factor * drawn, drawn)


def block_levels(own_key, shape, shards, low, top_value):
    level, own = 1.0, jax.random.fold_in(own_key, 6)
    for dim, parts in shards:
        heights = jnp.exp(jax.random.uniform(jax.random.fold_in(own, dim), (parts,), jnp.float32, low / len(shards), top_value / len(shards)))
        level = level * jnp.repeat(heights, shape[dim] // parts).reshape([-1 if axis == dim else 1 for axis in range(len(shape))])
    return level


def centred(key, dims, scale, reach, pieces=(), kind=jnp.bfloat16):
    result = jax.random.normal(key, dims, jnp.float32) * scale
    if len(pieces) > 0:
        result = block_levels(key, dims, pieces, -0.22, 0.18) * result
    return jnp.clip(result, min=-reach, max=reach).astype(kind)


def heavy_noise(stream_key, extent, deviation, bound, cuts, heavy, kind=jnp.bfloat16):
    values = deviation * jax.random.normal(stream_key, extent, jnp.float32)
    if cuts:
        values = values * block_levels(stream_key, extent, cuts, -0.22, 0.18)
    return jnp.clip(strengthened(values, jax.random.fold_in(stream_key, 3), *heavy), -bound, bound).astype(kind)


def setup_inputs(seed: int = 0, part: int = 0) -> dict:
    seeds = jax.random.split(jax.random.key(seed), 9)
    part_splits = jax.random.split(jax.random.fold_in(seeds[8], part), 9)
    activations = centred(part_splits[0], (TOKENS, D), 1.0, 6.0, ((0, 2), (1, 8)))
    cotangent = centred(part_splits[1], (TOKENS, FW), 1.0, 6.0, ((0, 2), (1, 8)))
    frozen_weight = heavy_noise(seeds[2], (D, FW), D ** -0.5, 0.09375, ((1, 8),), (1, 0, 8, 2.0))
    adapter_down = centred(seeds[3], (D, R), D ** -0.5, 0.0625, ((0, 8),))
    adapter_up = centred(seeds[4], (R, FW), R ** -0.5, 0.75, ((1, 8),))
    sparse_values = centred(seeds[5], (NBR, MAXR, BLK, BLK), BLK ** -0.5, 0.5, ((0, 8),))
    block_cols = draw_block_cols(jax.random.fold_in(seeds[8], 71), part)
    block_count = draw_block_count(jax.random.fold_in(seeds[8], 71), part)
    return dict(activations=activations, cotangent=cotangent, frozen_weight=frozen_weight, adapter_down=adapter_down, adapter_up=adapter_up, sparse_values=sparse_values, block_cols=block_cols, block_count=block_count)


adapter_scale = 0.125


def reference(activations, cotangent, frozen_weight, adapter_down, adapter_up, sparse_values, block_cols, block_count):
    loss_scale = TOKENS ** -0.5
    contract_last = (((1,), (1,)), ((), ()))
    contract_first = (((0,), (0,)), ((), ()))
    low = jnp.dot(activations, adapter_down, preferred_element_type=jnp.float32)
    low16 = low.astype(jnp.bfloat16)
    back = adapter_scale * lax.dot_general(cotangent, adapter_up, contract_last, preferred_element_type=jnp.float32)
    back16 = back.astype(jnp.bfloat16)
    down_grad = loss_scale * lax.dot_general(activations, back16, contract_first, preferred_element_type=jnp.float32)
    up_grad = (loss_scale * adapter_scale) * lax.dot_general(low16, cotangent, contract_first, preferred_element_type=jnp.float32)

    act_blocks = activations.reshape(TOKENS, NBR, BLK)
    cot_blocks = cotangent.reshape(TOKENS, NBC, BLK)
    slot_ids = jnp.arange(MAXR, dtype=jnp.int32)

    def per_row(row_id):
        row_cols = block_cols[row_id]
        used = (slot_ids < block_count[row_id]).astype(jnp.float32)
        act_row = lax.dynamic_index_in_dim(act_blocks, row_id, 1, keepdims=False).astype(jnp.float32)
        cot_row = jnp.take(cot_blocks, row_cols, axis=1).astype(jnp.float32)
        grads = loss_scale * jnp.einsum('tb,tkc->kbc', act_row, cot_row) * used[:, None, None]
        values = lax.dynamic_index_in_dim(sparse_values, row_id, 0, keepdims=False).astype(jnp.float32)
        values = values * used[:, None, None]
        term = jnp.einsum('tkc,kbc->tb', cot_row, values)
        return grads, term

    block_grads, sparse_rows = lax.map(per_row, jnp.arange(NBR, dtype=jnp.int32))
    sparse = jnp.transpose(sparse_rows, (1, 0, 2)).reshape(TOKENS, D)

    group_width = FW // N_MP
    dense = jnp.zeros((TOKENS, D), jnp.float32)
    for group in range(N_MP):
        piece_cot = cotangent[:, group * group_width:(group + 1) * group_width]
        piece_weight = frozen_weight[:, group * group_width:(group + 1) * group_width]
        partial_sum = lax.dot_general(piece_cot, piece_weight, contract_last, preferred_element_type=jnp.float32)
        rounded = lax.optimization_barrier(partial_sum.astype(jnp.bfloat16))
        dense = dense + rounded.astype(jnp.float32)

    adapter_term = lax.dot_general(back16, adapter_down, contract_last, preferred_element_type=jnp.float32)
    input_grad = (dense + sparse + adapter_term).astype(jnp.bfloat16)
    return input_grad, down_grad, up_grad, block_grads
```

```python
import functools

import jax
import jax.numpy as jnp
import numpy as np
from jax import lax
from jax.experimental import pallas as pl
from jax.experimental.pallas import tpu as pltpu
from jax.sharding import PartitionSpec as P

BLK = 128
MAXR = 8
CAP = 2
PIECE = 256
INNER = 2
MESH = pl.DeviceIdType.MESH

adapter_scale = 0.125
contract_last = (((1,), (1,)), ((), ()))
contract_first = (((0,), (0,)), ((), ()))


def slot_tables(block_cols, block_count, mp_count, per_owner, per_holder):
    col_table = block_cols.reshape(mp_count, per_owner * MAXR)
    slot_ids = jnp.tile(jnp.arange(MAXR, dtype=jnp.int32), per_owner)
    counts_wide = jnp.repeat(block_count.reshape(mp_count, per_owner), MAXR, axis=1)
    valid_slots = slot_ids[None, :] < counts_wide
    holder = col_table // per_holder
    block_ids = jnp.arange(per_owner * MAXR, dtype=jnp.int32)
    earlier = block_ids[None, :] < block_ids[:, None]
    same_holder = (
        (holder[:, :, None] == holder[:, None, :]) & valid_slots[:, None, :] & earlier[None, :, :]
    )
    slot_rank = jnp.sum(same_holder.astype(jnp.int32), axis=2)
    return (col_table, valid_slots, holder, slot_rank)


def outgoing(col_table, valid_slots, holder, slot_rank, my_index, per_holder):
    capacity_ids = jnp.arange(CAP, dtype=jnp.int32)
    picked = (
        valid_slots[:, :, None]
        & (holder == my_index)[:, :, None]
        & (slot_rank[:, :, None] == capacity_ids[None, None, :])
    )
    local_cols = (col_table - my_index * per_holder)[:, :, None]
    return jnp.sum(jnp.where(picked, local_cols, 0), axis=1).reshape(-1)


def orders(outer):
    rows = []
    for z in range(outer):
        rows.append(sorted(range(outer), key=lambda d: (-abs(d - z), (d - z) if z % 2 else (z - d))))
    return np.array(rows, np.int32)


def kernel(
    n,
    wanted_ref, index_ref, valid_ref,
    act_ref, cot_ref, w_ref, down_ref, up_ref, values_ref,
    out_ref, down_out, up_out, blocks_out,
    wbuf, ysend, yrecv, own, zrecv, cotb, colsend, colgot, cat, vcat, sparse, bgtmp, bgkeep, bgsend, bgrecv,
    lbpart, lbgot, lbfull, dsend, drecv, usend, urecv,
    wsem, ys_sem, yr_sem, zs_sem, zr_sem, cs_sem, cr_sem, l1s, l1r, l2s, l2r, dps, dpr,
):
    me = lax.axis_index("mp")
    core = lax.axis_index("dp")
    tok, wide = act_ref.shape
    outer = n // INNER
    pieces = wide // PIECE
    rows = wide // BLK
    part = tok // n
    z, y = me // INNER, me % INNER
    pair = z * INNER + (1 - y)
    loss_scale = (tok * 2) ** (-0.5)
    table = orders(outer)

    def pick(step):
        total = jnp.int32(0)
        for i in range(outer):
            for s in range(outer):
                total = total + jnp.where((z == i) & (step == s), jnp.int32(int(table[i, s])), 0)
        return total

    def remote(src, dst, send, recv, mp=None, dp=None):
        target = {"mp": mp} if dp is None else {"dp": dp}
        return pltpu.make_async_remote_copy(
            src_ref=src, dst_ref=dst, send_sem=send, recv_sem=recv,
            device_id=target, device_id_type=MESH,
        )

    barrier = pltpu.get_barrier_semaphore()
    for j in range(1, n):
        pl.semaphore_signal(
            barrier, inc=1, device_id={"mp": lax.rem(me + j, n)}, device_id_type=MESH
        )
    pl.semaphore_signal(barrier, inc=1, device_id={"dp": 1 - core}, device_id_type=MESH)

    def item_owner(i):
        far = i < outer
        zd = pick(jnp.where(far, i, i - outer))
        return zd, zd * INNER + jnp.where(far, 1 - y, y)

    def fetch(i):
        _, owner = item_owner(i)
        slot = lax.rem(i, 2)
        return pltpu.make_async_copy(
            w_ref.at[pl.ds(pl.multiple_of(owner * wide, wide), wide), :], wbuf.at[slot], wsem.at[slot]
        )

    fetch(jnp.int32(0)).start()
    fetch(jnp.int32(1)).start()

    low_part = jnp.dot(act_ref[...], down_ref[...], preferred_element_type=jnp.float32)
    back_part = lax.dot_general(
        cot_ref[...], up_ref[...], contract_last, preferred_element_type=jnp.float32
    )
    lbpart[:, :, 0:64] = low_part.astype(jnp.bfloat16).reshape(n, part, 64)
    lbpart[:, :, 64:128] = back_part.astype(jnp.bfloat16).reshape(n, part, 64)
    pl.semaphore_wait(barrier, n)

    def lb1(j):
        dest = lax.rem(me + j, n)
        return remote(lbpart.at[dest], lbgot.at[me], l1s.at[dest], l1r.at[me], mp=dest)

    def lb1_in(j):
        src = lax.rem(me + j, n)
        return remote(lbpart.at[src], lbgot.at[src], l1s.at[src], l1r.at[src], mp=src)

    def lb2(j):
        dest = lax.rem(me + j, n)
        return remote(lbfull.at[me], lbfull.at[me], l2s.at[dest], l2r.at[me], mp=dest)

    def lb2_in(j):
        src = lax.rem(me + j, n)
        return remote(lbfull.at[src], lbfull.at[src], l2s.at[src], l2r.at[src], mp=src)

    def cols(j):
        dest = lax.rem(me + j, n)
        return remote(
            colsend.at[pl.ds(dest * CAP, CAP)], colgot.at[pl.ds(me * CAP, CAP)],
            cs_sem.at[dest], cr_sem.at[me], mp=dest,
        )

    def cols_in(j):
        src = lax.rem(me + j, n)
        return remote(
            colsend.at[pl.ds(src * CAP, CAP)], colgot.at[pl.ds(src * CAP, CAP)],
            cs_sem.at[src], cr_sem.at[src], mp=src,
        )

    def loop(count, body, start=0):
        def step(i, carry):
            body(i)
            return carry

        lax.fori_loop(start, count, step, 0)

    loop(n, lambda j: lb1(j).start(), 1)

    for i in range(cotb.shape[0]):
        cotb[i] = cot_ref[:, i * BLK:(i + 1) * BLK]

    def send_cols(j):
        dest = lax.rem(me + j, n)
        for q in range(CAP):
            colsend[dest * CAP + q] = cotb[wanted_ref[dest * CAP + q]]
        cols(j).start()

    def pair_copy(zd, c):
        return remote(ysend.at[zd, c], yrecv.at[zd, c], ys_sem.at[zd, c], yr_sem.at[zd, c], mp=pair)

    def product(slot, c):
        return lax.dot_general(
            cot_ref[...], wbuf[slot, pl.ds(pl.multiple_of(c * PIECE, PIECE), PIECE), :],
            contract_last, preferred_element_type=jnp.float32,
        ).astype(jnp.bfloat16)

    def refill(i):
        @pl.when(i + 2 < 2 * outer)
        def _():
            fetch(i + 2).start()

    def far_item(i):
        zd, _ = item_owner(i)
        slot = lax.rem(i, 2)
        fetch(i).wait()

        def one(c):
            ysend[zd, c] = product(slot, c)
            pair_copy(zd, c).start()

        loop(pieces, one)
        refill(i)

    def near_item(i):
        zd, _ = item_owner(i)
        slot = lax.rem(i, 2)
        fetch(i).wait()

        def one(c):
            own[zd, c] = product(slot, c)

        loop(pieces, one)
        refill(i)

    far_item(jnp.int32(0))
    loop(n, send_cols, 1)
    for q in range(CAP):
        colgot[me * CAP + q] = cotb[wanted_ref[me * CAP + q]]
    loop(outer, far_item, 1)

    loop(n, lambda j: lb1_in(j).wait_recv(), 1)
    lbgot[me] = lbpart[me]
    total = lbgot[0].astype(jnp.float32)
    for i in range(1, n):
        total = total + lbgot[i].astype(jnp.float32)
    lbfull[me] = total.astype(jnp.bfloat16)
    loop(n, lambda j: lb2(j).start(), 1)

    loop(2 * outer, near_item, outer)

    def up_copy(zd, c):
        return remote(own.at[zd, c], zrecv.at[zd, c], zs_sem.at[zd, c], zr_sem.at[zd, c], mp=me + INNER)

    def down_copy(zd, c):
        slot = jnp.where(zd == z - 1, outer, zd)
        return remote(own.at[zd, c], zrecv.at[slot, c], zs_sem.at[zd, c], zr_sem.at[slot, c], mp=me - INNER)

    def chain_in(slot, c):
        return remote(own.at[0, c], zrecv.at[slot, c], zs_sem.at[0, c], zr_sem.at[slot, c], mp=pair)

    def forward(s):
        zd = pick(s)
        incoming = ((zd > z) & (z > 0)) | ((zd < z) & (z < outer - 1))

        def one(c):
            pair_copy(zd, c).wait_recv()
            acc = own[zd, c].astype(jnp.float32) + yrecv[zd, c].astype(jnp.float32)

            @pl.when(incoming)
            def _():
                chain_in(zd, c).wait_recv()
                own[zd, c] = (acc + zrecv[zd, c].astype(jnp.float32)).astype(jnp.bfloat16)

            @pl.when(jnp.logical_not(incoming))
            def _():
                own[zd, c] = acc.astype(jnp.bfloat16)

            @pl.when(zd > z)
            def _():
                up_copy(zd, c).start()

            @pl.when(zd < z)
            def _():
                down_copy(zd, c).start()

        loop(pieces, one)

    loop(outer - 1, forward)

    loop(n, lambda j: lb2_in(j).wait_recv(), 1)
    both = lbfull[...].reshape(tok, 128)
    low16 = both[:, 0:64]
    back16 = (adapter_scale * both[:, 64:128].astype(jnp.float32)).astype(jnp.bfloat16)

    def dcopy():
        return remote(dsend, drecv, dps.at[0], dpr.at[0], dp=1 - core)

    def ucopy():
        return remote(usend, urecv, dps.at[1], dpr.at[1], dp=1 - core)

    def bcopy(a):
        return remote(bgsend.at[a], bgrecv.at[a], dps.at[2 + a], dpr.at[2 + a], dp=1 - core)

    dsend[...] = (
        loss_scale
        * lax.dot_general(act_ref[...], back16, contract_first, preferred_element_type=jnp.float32)
    ).astype(jnp.bfloat16)
    dcopy().start()
    usend[...] = (
        loss_scale
        * adapter_scale
        * lax.dot_general(low16, cot_ref[...], contract_first, preferred_element_type=jnp.float32)
    ).astype(jnp.bfloat16)
    ucopy().start()

    loop(n, lambda j: cols_in(j).wait_recv(), 1)
    half = MAXR * BLK // 2

    def block_row(a):
        for k in range(MAXR):
            lanes = slice(k * BLK, (k + 1) * BLK)
            cat[:, lanes] = colgot[index_ref[a * MAXR + k]] * valid_ref[a, :, lanes]
            vcat[:, k * BLK:(k + 1) * BLK] = values_ref[a, k]
        first = pl.multiple_of(a * BLK, BLK)
        act_row = act_ref[:, pl.ds(first, BLK)]
        bgtmp[...] = loss_scale * lax.dot_general(
            act_row, cat[...], contract_first, preferred_element_type=jnp.float32
        )
        bgkeep[a] = bgtmp[:, pl.ds(pl.multiple_of(core * half, half), half)]
        bgsend[a] = bgtmp[:, pl.ds(pl.multiple_of((1 - core) * half, half), half)].astype(jnp.bfloat16)
        bcopy(a).start()
        sparse[:, pl.ds(first, BLK)] = lax.dot_general(
            cat[...], vcat[...], contract_last, preferred_element_type=jnp.float32
        ) + lax.dot_general(
            back16, down_ref[pl.ds(first, BLK), :], contract_last, preferred_element_type=jnp.float32
        )

    loop(rows, block_row)

    dcopy().wait_recv()
    ucopy().wait_recv()
    down_out[...] = dsend[...].astype(jnp.float32) + drecv[...].astype(jnp.float32)
    up_out[...] = usend[...].astype(jnp.float32) + urecv[...].astype(jnp.float32)

    def block_sum(a):
        bcopy(a).wait_recv()
        for k in range(MAXR // 2):
            lanes = slice(k * BLK, (k + 1) * BLK)
            blocks_out[a, k] = bgkeep[a, :, lanes] + bgrecv[a, :, lanes].astype(jnp.float32)

    loop(rows, block_sum)

    def last(c):
        lanes = pl.ds(pl.multiple_of(c * PIECE, PIECE), PIECE)
        pair_copy(z, c).wait_recv()
        sparse[:, lanes] += own[z, c].astype(jnp.float32) + yrecv[z, c].astype(jnp.float32)

        @pl.when(z > 0)
        def _():
            chain_in(z, c).wait_recv()
            sparse[:, lanes] += zrecv[z, c].astype(jnp.float32)

        @pl.when(z < outer - 1)
        def _():
            chain_in(outer, c).wait_recv()
            sparse[:, lanes] += zrecv[outer, c].astype(jnp.float32)

        out_ref[:, lanes] = sparse[:, lanes].astype(jnp.bfloat16)

    loop(pieces, last)

    def drain(s):
        def one(c):
            pair_copy(s, c).wait_send()

            @pl.when(s > z)
            def _():
                up_copy(s, c).wait_send()

            @pl.when(s < z)
            def _():
                down_copy(s, c).wait_send()

        loop(pieces, one)

    loop(outer, drain)

    def drain_small(j):
        lb1(j).wait_send()
        lb2(j).wait_send()
        cols(j).wait_send()

    loop(n, drain_small, 1)
    dcopy().wait_send()
    ucopy().wait_send()
    loop(rows, lambda a: bcopy(a).wait_send())


def local(
    activations,
    cotangent,
    frozen_weight,
    adapter_down,
    adapter_up,
    sparse_values,
    block_cols,
    block_count,
):
    tok, wide = activations.shape
    hidden = cotangent.shape[1]
    n = lax.axis_size("mp")
    me = lax.axis_index("mp")
    per_owner = wide // BLK
    per_holder = hidden // BLK
    col_table, valid_slots, holder, slot_rank = slot_tables(
        block_cols, block_count, n, per_owner, per_holder
    )
    my_valid = lax.dynamic_index_in_dim(valid_slots, me, 0, keepdims=False)
    my_holder = lax.dynamic_index_in_dim(holder, me, 0, keepdims=False)
    my_rank = lax.dynamic_index_in_dim(slot_rank, me, 0, keepdims=False)
    recv_index = jnp.where(my_valid, my_holder * CAP + jnp.minimum(my_rank, CAP - 1), 0)
    wanted = outgoing(col_table, valid_slots, holder, slot_rank, me, per_holder)

    outer = n // INNER
    pieces = wide // PIECE
    part = tok // n
    bf, f32 = jnp.bfloat16, jnp.float32
    half = MAXR * BLK // 2
    vmem = pl.BlockSpec(memory_space=pltpu.VMEM)
    smem = pl.BlockSpec(memory_space=pltpu.SMEM)
    dma = pltpu.SemaphoreType.DMA
    return pl.pallas_call(
        functools.partial(kernel, n),
        out_shape=(
            jax.ShapeDtypeStruct((tok, wide), bf),
            jax.ShapeDtypeStruct((wide, 64), f32),
            jax.ShapeDtypeStruct((64, hidden), f32),
            jax.ShapeDtypeStruct((per_owner, MAXR // 2, BLK, BLK), f32),
        ),
        in_specs=[smem, smem, vmem, vmem, vmem, pl.BlockSpec(memory_space=pl.ANY), vmem, vmem, vmem],
        out_specs=(vmem, vmem, vmem, vmem),
        scratch_shapes=[
            pltpu.VMEM((2, wide, hidden), bf),
            pltpu.VMEM((outer, pieces, tok, PIECE), bf),
            pltpu.VMEM((outer, pieces, tok, PIECE), bf),
            pltpu.VMEM((outer, pieces, tok, PIECE), bf),
            pltpu.VMEM((outer + 1, pieces, tok, PIECE), bf),
            pltpu.VMEM((per_holder, tok, BLK), bf),
            pltpu.VMEM((n * CAP, tok, BLK), bf),
            pltpu.VMEM((n * CAP, tok, BLK), bf),
            pltpu.VMEM((tok, MAXR * BLK), bf),
            pltpu.VMEM((BLK, MAXR * BLK), bf),
            pltpu.VMEM((tok, wide), f32),
            pltpu.VMEM((BLK, MAXR * BLK), f32),
            pltpu.VMEM((per_owner, BLK, half), f32),
            pltpu.VMEM((per_owner, BLK, half), bf),
            pltpu.VMEM((per_owner, BLK, half), bf),
            pltpu.VMEM((n, part, 128), bf),
            pltpu.VMEM((n, part, 128), bf),
            pltpu.VMEM((n, part, 128), bf),
            pltpu.VMEM((wide, 64), bf),
            pltpu.VMEM((wide, 64), bf),
            pltpu.VMEM((64, hidden), bf),
            pltpu.VMEM((64, hidden), bf),
            dma((2,)),
            dma((outer, pieces)),
            dma((outer, pieces)),
            dma((outer, pieces)),
            dma((outer + 1, pieces)),
            dma((n,)),
            dma((n,)),
            dma((n,)),
            dma((n,)),
            dma((n,)),
            dma((n,)),
            dma((2 + per_owner,)),
            dma((2 + per_owner,)),
        ],
        compiler_params=pltpu.CompilerParams(
            collective_id=0, has_side_effects=True, vmem_limit_bytes=60 * 1024 * 1024
        ),
    )(
        wanted.astype(jnp.int32),
        recv_index.astype(jnp.int32),
        jnp.repeat(my_valid.reshape(per_owner, 1, MAXR).astype(bf), BLK, axis=2),
        activations,
        cotangent,
        frozen_weight,
        adapter_down,
        adapter_up,
        sparse_values,
    )


def solution(mesh):
    return jax.shard_map(
        local,
        mesh=mesh,
        in_specs=(
            P(("groups", "dp"), "mp"),
            P(("groups", "dp"), "mp"),
            P(None, "mp"),
            P("mp", None),
            P(None, "mp"),
            P("mp", None, None, None),
            P(),
            P(),
        ),
        out_specs=(
            P(("groups", "dp"), "mp"),
            P(("groups", "mp"), None),
            P("groups", "mp"),
            P(("groups", "mp"), "dp", None, None),
        ),
        check_vma=False,
    )
```

```python
import functools

import jax
import jax.numpy as jnp
import numpy as np
from jax import lax
from jax.experimental import pallas as pl
from jax.experimental.pallas import tpu as pltpu
from jax.sharding import PartitionSpec as P

BLK = 128
MAXR = 8
CAP = 2
PIECE = 256
INNER = 2
MESH = pl.DeviceIdType.MESH

adapter_scale = 0.125
contract_last = (((1,), (1,)), ((), ()))
contract_first = (((0,), (0,)), ((), ()))


def orders(outer):
    rows = []
    for z in range(outer):
        rows.append(sorted(range(outer), key=lambda d: (-abs(d - z), (d - z) if z % 2 else (z - d))))
    return np.array(rows, np.int32)


def kernel(
    n,
    cols_ref, count_ref,
    act_ref, cot_ref, w_ref, down_ref, up_ref, values_hbm,
    out_ref, down_out, up_out, blocks_out,
    values_ref, index_ref, wbuf, ysend, yrecv, own, zrecv, cotb, colsend, colgot, cat, vcat, sparse, bgtmp, bgkeep, bgsend, bgrecv,
    lbpart, lbgot, lbfull, dsend, drecv, usend, urecv,
    vsem, wsem, ys_sem, yr_sem, zs_sem, zr_sem, cs_sem, cr_sem, l1s, l1r, l2s, l2r, dps, dpr,
):
    me = lax.axis_index("mp")
    core = lax.axis_index("dp")
    tok, wide = act_ref.shape
    outer = n // INNER
    pieces = wide // PIECE
    rows = wide // BLK
    part = tok // n
    z, y = me // INNER, me % INNER
    pair = z * INNER + (1 - y)
    loss_scale = (tok * 2) ** (-0.5)
    table = orders(outer)

    def pick(step):
        total = jnp.int32(0)
        for i in range(outer):
            for s in range(outer):
                total = total + jnp.where((z == i) & (step == s), jnp.int32(int(table[i, s])), 0)
        return total

    def remote(src, dst, send, recv, mp=None, dp=None):
        target = {"mp": mp} if dp is None else {"dp": dp}
        return pltpu.make_async_remote_copy(
            src_ref=src, dst_ref=dst, send_sem=send, recv_sem=recv,
            device_id=target, device_id_type=MESH,
        )

    barrier = pltpu.get_barrier_semaphore()
    for j in range(1, n):
        pl.semaphore_signal(
            barrier, inc=1, device_id={"mp": lax.rem(me + j, n)}, device_id_type=MESH
        )
    pl.semaphore_signal(barrier, inc=1, device_id={"dp": 1 - core}, device_id_type=MESH)

    def item_owner(i):
        far = i < outer
        zd = pick(jnp.where(far, i, i - outer))
        return zd, zd * INNER + jnp.where(far, 1 - y, y)

    def fetch(i):
        _, owner = item_owner(i)
        slot = lax.rem(i, 2)
        return pltpu.make_async_copy(
            w_ref.at[pl.ds(pl.multiple_of(owner * wide, wide), wide), :], wbuf.at[slot], wsem.at[slot]
        )

    fetch(jnp.int32(0)).start()
    fetch(jnp.int32(1)).start()

    values_in = pltpu.make_async_copy(values_hbm, values_ref, vsem.at[0])
    values_in.start()
    low_part = lax.dot_general(
        act_ref[...], down_ref[...], contract_last, preferred_element_type=jnp.float32
    )
    back_part = lax.dot_general(
        cot_ref[...], up_ref[...], contract_last, preferred_element_type=jnp.float32
    )
    lbpart[:, :, 0:64] = low_part.astype(jnp.bfloat16).reshape(n, part, 64)
    lbpart[:, :, 64:128] = back_part.astype(jnp.bfloat16).reshape(n, part, 64)
    pl.semaphore_wait(barrier, n)

    def lb1(j):
        dest = lax.rem(me + j, n)
        return remote(lbpart.at[dest], lbgot.at[me], l1s.at[dest], l1r.at[me], mp=dest)

    def lb1_in(j):
        src = lax.rem(me + j, n)
        return remote(lbpart.at[src], lbgot.at[src], l1s.at[src], l1r.at[src], mp=src)

    def lb2(j):
        dest = lax.rem(me + j, n)
        return remote(lbfull.at[me], lbfull.at[me], l2s.at[dest], l2r.at[me], mp=dest)

    def lb2_in(j):
        src = lax.rem(me + j, n)
        return remote(lbfull.at[src], lbfull.at[src], l2s.at[src], l2r.at[src], mp=src)

    def cols(j):
        dest = lax.rem(me + j, n)
        return remote(
            colsend.at[pl.ds(dest * CAP, CAP)], colgot.at[pl.ds(me * CAP, CAP)],
            cs_sem.at[dest], cr_sem.at[me], mp=dest,
        )

    def cols_in(j):
        src = lax.rem(me + j, n)
        return remote(
            colsend.at[pl.ds(src * CAP, CAP)], colgot.at[pl.ds(src * CAP, CAP)],
            cs_sem.at[src], cr_sem.at[src], mp=src,
        )

    def loop(count, body, start=0):
        def step(i, carry):
            body(i)
            return carry

        lax.fori_loop(start, count, step, 0)

    loop(n, lambda j: lb1(j).start(), 1)

    for i in range(cotb.shape[0]):
        cotb[i] = cot_ref[:, i * BLK:(i + 1) * BLK]

    holders = cotb.shape[0]
    shape = cols_ref.shape
    slot_ids = lax.broadcasted_iota(jnp.int32, shape, 0)
    row_ids = lax.broadcasted_iota(jnp.int32, shape, 1)
    block_ids = slot_ids * shape[1] + row_ids
    block_at = cols_ref[...]
    used = slot_ids < count_ref[...]
    far_code = jnp.int32(1 << 30)

    def held(first_row, holder):
        inside = (row_ids >= first_row) & (row_ids < first_row + rows)
        return used & inside & (block_at >= holder * holders) & (block_at < (holder + 1) * holders)

    def wanted(dest):
        mine = held(dest * rows, me)
        code = block_ids * BLK + (block_at - me * holders)
        low_code = jnp.min(jnp.where(mine, code, far_code))
        high_code = jnp.max(jnp.where(mine, code, 0))
        return (low_code & (BLK - 1), high_code & (BLK - 1))

    def send_cols(j):
        dest = lax.rem(me + j, n)
        for q, at in enumerate(wanted(dest)):
            colsend[dest * CAP + q] = cotb[at]
        cols(j).start()

    def pair_copy(zd, c):
        return remote(ysend.at[zd, c], yrecv.at[zd, c], ys_sem.at[zd, c], yr_sem.at[zd, c], mp=pair)

    def product(slot, c):
        return lax.dot_general(
            cot_ref[...], wbuf[slot, pl.ds(pl.multiple_of(c * PIECE, PIECE), PIECE), :],
            contract_last, preferred_element_type=jnp.float32,
        ).astype(jnp.bfloat16)

    def refill(i):
        @pl.when(i + 2 < 2 * outer)
        def _():
            fetch(i + 2).start()

    def far_item(i):
        zd, _ = item_owner(i)
        slot = lax.rem(i, 2)
        fetch(i).wait()

        def one(c):
            ysend[zd, c] = product(slot, c)
            pair_copy(zd, c).start()

        loop(pieces, one)
        refill(i)

    def near_item(i):
        zd, _ = item_owner(i)
        slot = lax.rem(i, 2)
        fetch(i).wait()

        def one(c):
            own[zd, c] = product(slot, c)

        loop(pieces, one)
        refill(i)

    far_item(jnp.int32(0))
    loop(n, send_cols, 1)
    for q, at in enumerate(wanted(me)):
        colgot[me * CAP + q] = cotb[at]
    colgot[n * CAP] = jnp.zeros((tok, BLK), jnp.bfloat16)
    loop(outer, far_item, 1)

    loop(n, lambda j: lb1_in(j).wait_recv(), 1)
    lbgot[me] = lbpart[me]
    total = lbgot[0].astype(jnp.float32)
    for i in range(1, n):
        total = total + lbgot[i].astype(jnp.float32)
    lbfull[me] = total.astype(jnp.bfloat16)
    loop(n, lambda j: lb2(j).start(), 1)

    loop(2 * outer, near_item, outer)

    def up_copy(zd, c):
        return remote(own.at[zd, c], zrecv.at[zd, c], zs_sem.at[zd, c], zr_sem.at[zd, c], mp=me + INNER)

    def down_copy(zd, c):
        slot = jnp.where(zd == z - 1, outer, zd)
        return remote(own.at[zd, c], zrecv.at[slot, c], zs_sem.at[zd, c], zr_sem.at[slot, c], mp=me - INNER)

    def chain_in(slot, c):
        return remote(own.at[0, c], zrecv.at[slot, c], zs_sem.at[0, c], zr_sem.at[slot, c], mp=pair)

    def forward(s):
        zd = pick(s)
        incoming = ((zd > z) & (z > 0)) | ((zd < z) & (z < outer - 1))

        def one(c):
            pair_copy(zd, c).wait_recv()
            acc = own[zd, c].astype(jnp.float32) + yrecv[zd, c].astype(jnp.float32)

            @pl.when(incoming)
            def _():
                chain_in(zd, c).wait_recv()
                own[zd, c] = (acc + zrecv[zd, c].astype(jnp.float32)).astype(jnp.bfloat16)

            @pl.when(jnp.logical_not(incoming))
            def _():
                own[zd, c] = acc.astype(jnp.bfloat16)

            @pl.when(zd > z)
            def _():
                up_copy(zd, c).start()

            @pl.when(zd < z)
            def _():
                down_copy(zd, c).start()

        loop(pieces, one)

    loop(outer - 1, forward)

    index_ref[...] = jnp.full(shape, n * CAP, jnp.int32)

    def place(holder):
        mine = held(me * rows, holder)
        first = jnp.min(jnp.where(mine, block_ids, far_code))
        rank = jnp.where(block_ids > first, 1, 0)
        index_ref[...] = jnp.where(mine, holder * CAP + rank, index_ref[...])

    loop(n, place)

    loop(n, lambda j: lb2_in(j).wait_recv(), 1)
    both = lbfull[...].reshape(tok, 128)
    low16 = both[:, 0:64]
    back16 = (adapter_scale * both[:, 64:128].astype(jnp.float32)).astype(jnp.bfloat16)

    def dcopy():
        return remote(dsend, drecv, dps.at[0], dpr.at[0], dp=1 - core)

    def ucopy():
        return remote(usend, urecv, dps.at[1], dpr.at[1], dp=1 - core)

    def bcopy(a):
        return remote(bgsend.at[a], bgrecv.at[a], dps.at[2 + a], dpr.at[2 + a], dp=1 - core)

    dsend[...] = (
        loss_scale
        * lax.dot_general(back16, act_ref[...], contract_first, preferred_element_type=jnp.float32)
    ).astype(jnp.bfloat16)
    dcopy().start()
    usend[...] = (
        loss_scale
        * adapter_scale
        * lax.dot_general(low16, cot_ref[...], contract_first, preferred_element_type=jnp.float32)
    ).astype(jnp.bfloat16)
    ucopy().start()

    values_in.wait()
    loop(n, lambda j: cols_in(j).wait_recv(), 1)
    half = MAXR * BLK // 2

    def block_row(a):
        for k in range(MAXR):
            lanes = slice(k * BLK, (k + 1) * BLK)
            here = (slot_ids == k) & (row_ids == me * rows + a)
            cat[:, lanes] = colgot[jnp.sum(jnp.where(here, index_ref[...], 0))]
            vcat[:, k * BLK:(k + 1) * BLK] = values_ref[a, k]
        first = pl.multiple_of(a * BLK, BLK)
        act_row = act_ref[:, pl.ds(first, BLK)]
        bgtmp[...] = loss_scale * lax.dot_general(
            act_row, cat[...], contract_first, preferred_element_type=jnp.float32
        )
        bgkeep[a] = bgtmp[:, pl.ds(pl.multiple_of(core * half, half), half)]
        bgsend[a] = bgtmp[:, pl.ds(pl.multiple_of((1 - core) * half, half), half)].astype(jnp.bfloat16)
        bcopy(a).start()
        sparse[:, pl.ds(first, BLK)] = lax.dot_general(
            cat[...], vcat[...], contract_last, preferred_element_type=jnp.float32
        ) + jnp.dot(back16, down_ref[:, pl.ds(first, BLK)], preferred_element_type=jnp.float32)

    loop(rows, block_row)

    dcopy().wait_recv()
    ucopy().wait_recv()
    down_out[...] = dsend[...].astype(jnp.float32) + drecv[...].astype(jnp.float32)
    up_out[...] = usend[...].astype(jnp.float32) + urecv[...].astype(jnp.float32)

    def block_sum(a):
        bcopy(a).wait_recv()
        for k in range(MAXR // 2):
            lanes = slice(k * BLK, (k + 1) * BLK)
            blocks_out[a, k] = bgkeep[a, :, lanes] + bgrecv[a, :, lanes].astype(jnp.float32)

    loop(rows, block_sum)

    def last(c):
        lanes = pl.ds(pl.multiple_of(c * PIECE, PIECE), PIECE)
        pair_copy(z, c).wait_recv()
        sparse[:, lanes] += own[z, c].astype(jnp.float32) + yrecv[z, c].astype(jnp.float32)

        @pl.when(z > 0)
        def _():
            chain_in(z, c).wait_recv()
            sparse[:, lanes] += zrecv[z, c].astype(jnp.float32)

        @pl.when(z < outer - 1)
        def _():
            chain_in(outer, c).wait_recv()
            sparse[:, lanes] += zrecv[outer, c].astype(jnp.float32)

        out_ref[:, lanes] = sparse[:, lanes].astype(jnp.bfloat16)

    loop(pieces, last)

    def drain(s):
        def one(c):
            pair_copy(s, c).wait_send()

            @pl.when(s > z)
            def _():
                up_copy(s, c).wait_send()

            @pl.when(s < z)
            def _():
                down_copy(s, c).wait_send()

        loop(pieces, one)

    loop(outer, drain)

    def drain_small(j):
        lb1(j).wait_send()
        lb2(j).wait_send()
        cols(j).wait_send()

    loop(n, drain_small, 1)
    dcopy().wait_send()
    ucopy().wait_send()
    loop(rows, lambda a: bcopy(a).wait_send())


def local(
    activations,
    cotangent,
    frozen_weight,
    adapter_down,
    adapter_up,
    sparse_values,
    block_cols,
    block_count,
):
    tok, wide = activations.shape
    hidden = cotangent.shape[1]
    n = lax.axis_size("mp")
    per_owner = wide // BLK
    per_holder = hidden // BLK
    outer = n // INNER
    pieces = wide // PIECE
    part = tok // n
    bf, f32 = jnp.bfloat16, jnp.float32
    half = MAXR * BLK // 2
    vmem = pl.BlockSpec(memory_space=pltpu.VMEM)
    anywhere = pl.BlockSpec(memory_space=pl.ANY)
    dma = pltpu.SemaphoreType.DMA
    input_grad, down_turned, up_grad, block_grads = pl.pallas_call(
        functools.partial(kernel, n),
        out_shape=(
            jax.ShapeDtypeStruct((tok, wide), bf),
            jax.ShapeDtypeStruct((64, wide), f32),
            jax.ShapeDtypeStruct((64, hidden), f32),
            jax.ShapeDtypeStruct((per_owner, MAXR // 2, BLK, BLK), f32),
        ),
        in_specs=[vmem, vmem, vmem, vmem, anywhere, vmem, vmem, anywhere],
        out_specs=(vmem, vmem, vmem, vmem),
        scratch_shapes=[
            pltpu.VMEM(sparse_values.shape, bf),
            pltpu.VMEM(block_cols.shape[::-1], jnp.int32),
            pltpu.VMEM((2, wide, hidden), bf),
            pltpu.VMEM((outer, pieces, tok, PIECE), bf),
            pltpu.VMEM((outer, pieces, tok, PIECE), bf),
            pltpu.VMEM((outer, pieces, tok, PIECE), bf),
            pltpu.VMEM((outer + 1, pieces, tok, PIECE), bf),
            pltpu.VMEM((per_holder, tok, BLK), bf),
            pltpu.VMEM((n * CAP, tok, BLK), bf),
            pltpu.VMEM((n * CAP + 1, tok, BLK), bf),
            pltpu.VMEM((tok, MAXR * BLK), bf),
            pltpu.VMEM((BLK, MAXR * BLK), bf),
            pltpu.VMEM((tok, wide), f32),
            pltpu.VMEM((BLK, MAXR * BLK), f32),
            pltpu.VMEM((per_owner, BLK, half), f32),
            pltpu.VMEM((per_owner, BLK, half), bf),
            pltpu.VMEM((per_owner, BLK, half), bf),
            pltpu.VMEM((n, part, 128), bf),
            pltpu.VMEM((n, part, 128), bf),
            pltpu.VMEM((n, part, 128), bf),
            pltpu.VMEM((64, wide), bf),
            pltpu.VMEM((64, wide), bf),
            pltpu.VMEM((64, hidden), bf),
            pltpu.VMEM((64, hidden), bf),
            dma((1,)),
            dma((2,)),
            dma((outer, pieces)),
            dma((outer, pieces)),
            dma((outer, pieces)),
            dma((outer + 1, pieces)),
            dma((n,)),
            dma((n,)),
            dma((n,)),
            dma((n,)),
            dma((n,)),
            dma((n,)),
            dma((2 + per_owner,)),
            dma((2 + per_owner,)),
        ],
        compiler_params=pltpu.CompilerParams(
            collective_id=0, has_side_effects=True, vmem_limit_bytes=60 * 1024 * 1024
        ),
    )(
        block_cols.T,
        block_count.reshape(1, -1),
        activations,
        cotangent,
        frozen_weight,
        adapter_down.T,
        adapter_up,
        sparse_values,
    )
    return input_grad, down_turned.T, up_grad, block_grads


def solution(mesh):
    return jax.shard_map(
        local,
        mesh=mesh,
        in_specs=(
            P(("groups", "dp"), "mp"),
            P(("groups", "dp"), "mp"),
            P(None, "mp"),
            P("mp", None),
            P(None, "mp"),
            P("mp", None, None, None),
            P(),
            P(),
        ),
        out_specs=(
            P(("groups", "dp"), "mp"),
            P(("groups", "mp"), None),
            P("groups", "mp"),
            P(("groups", "mp"), "dp", None, None),
        ),
        check_vma=False,
    )
```

```python
import functools

import jax
import jax.numpy as jnp
import numpy as np
from jax import lax
from jax.experimental import pallas as pl
from jax.experimental.pallas import tpu as pltpu
from jax.sharding import PartitionSpec as P

BLK = 128
MAXR = 8
CAP = 2
PIECE = 256
INNER = 2
MESH = pl.DeviceIdType.MESH

adapter_scale = 0.125
contract_last = (((1,), (1,)), ((), ()))
contract_first = (((0,), (0,)), ((), ()))


def orders(outer):
    rows = []
    for z in range(outer):
        rows.append(sorted(range(outer), key=lambda d: (-abs(d - z), (d - z) if z % 2 else (z - d))))
    return np.array(rows, np.int32)


def kernel(
    n,
    cols_ref, count_ref,
    act_ref, cot_ref, w_ref, down_ref, up_ref, values_hbm,
    out_ref, down_out, up_out, blocks_out,
    values_ref, index_ref, wbuf, ysend, yrecv, own, zrecv, crossrecv, cotb, colsend, colgot, cat, vcat, sparse, bgtmp, bgkeep, bgsend, bgrecv,
    lbpart, lbgot, lbfull, dsend, drecv, usend, urecv,
    vsem, wsem, ys_sem, yr_sem, zs_sem, zr_sem, xs_sem, xr_sem, cs_sem, cr_sem, l1s, l1r, l2s, l2r, dps, dpr,
):
    me = lax.axis_index("mp")
    core = lax.axis_index("dp")
    tok, wide = act_ref.shape
    outer = n // INNER
    pieces = wide // PIECE
    rows = wide // BLK
    part = tok // n
    z, y = me // INNER, me % INNER
    pair = z * INNER + (1 - y)
    loss_scale = (tok * 2) ** (-0.5)
    table = orders(outer)

    def pick(step):
        total = jnp.int32(0)
        for i in range(outer):
            for s in range(outer):
                total = total + jnp.where((z == i) & (step == s), jnp.int32(int(table[i, s])), 0)
        return total

    def remote(src, dst, send, recv, mp=None, dp=None):
        target = {"mp": mp} if dp is None else {"dp": dp}
        return pltpu.make_async_remote_copy(
            src_ref=src, dst_ref=dst, send_sem=send, recv_sem=recv,
            device_id=target, device_id_type=MESH,
        )

    barrier = pltpu.get_barrier_semaphore()
    for j in range(1, n):
        pl.semaphore_signal(
            barrier, inc=1, device_id={"mp": lax.rem(me + j, n)}, device_id_type=MESH
        )
    pl.semaphore_signal(barrier, inc=1, device_id={"dp": 1 - core}, device_id_type=MESH)

    def item_owner(i):
        far = i < outer
        zd = pick(jnp.where(far, i, i - outer))
        return zd, zd * INNER + jnp.where(far, 1 - y, y)

    def fetch(i):
        _, owner = item_owner(i)
        slot = lax.rem(i, 2)
        return pltpu.make_async_copy(
            w_ref.at[pl.ds(pl.multiple_of(owner * wide, wide), wide), :], wbuf.at[slot], wsem.at[slot]
        )

    fetch(jnp.int32(0)).start()
    fetch(jnp.int32(1)).start()

    values_in = pltpu.make_async_copy(values_hbm, values_ref, vsem.at[0])
    values_in.start()
    low_part = lax.dot_general(
        act_ref[...], down_ref[...], contract_last, preferred_element_type=jnp.float32
    )
    back_part = lax.dot_general(
        cot_ref[...], up_ref[...], contract_last, preferred_element_type=jnp.float32
    )
    lbpart[:, :, 0:64] = low_part.astype(jnp.bfloat16).reshape(n, part, 64)
    lbpart[:, :, 64:128] = back_part.astype(jnp.bfloat16).reshape(n, part, 64)
    pl.semaphore_wait(barrier, n)

    def lb1(j):
        dest = lax.rem(me + j, n)
        return remote(lbpart.at[dest], lbgot.at[me], l1s.at[dest], l1r.at[me], mp=dest)

    def lb1_in(j):
        src = lax.rem(me + j, n)
        return remote(lbpart.at[src], lbgot.at[src], l1s.at[src], l1r.at[src], mp=src)

    def lb2(j):
        dest = lax.rem(me + j, n)
        return remote(lbfull.at[me], lbfull.at[me], l2s.at[dest], l2r.at[me], mp=dest)

    def lb2_in(j):
        src = lax.rem(me + j, n)
        return remote(lbfull.at[src], lbfull.at[src], l2s.at[src], l2r.at[src], mp=src)

    def cols(j):
        dest = lax.rem(me + j, n)
        return remote(
            colsend.at[pl.ds(dest * CAP, CAP)], colgot.at[pl.ds(me * CAP, CAP)],
            cs_sem.at[dest], cr_sem.at[me], mp=dest,
        )

    def cols_in(j):
        src = lax.rem(me + j, n)
        return remote(
            colsend.at[pl.ds(src * CAP, CAP)], colgot.at[pl.ds(src * CAP, CAP)],
            cs_sem.at[src], cr_sem.at[src], mp=src,
        )

    def loop(count, body, start=0):
        def step(i, carry):
            body(i)
            return carry

        lax.fori_loop(start, count, step, 0)

    loop(n, lambda j: lb1(j).start(), 1)

    for i in range(cotb.shape[0]):
        cotb[i] = cot_ref[:, i * BLK:(i + 1) * BLK]

    holders = cotb.shape[0]
    shape = cols_ref.shape
    slot_ids = lax.broadcasted_iota(jnp.int32, shape, 0)
    row_ids = lax.broadcasted_iota(jnp.int32, shape, 1)
    block_ids = slot_ids * shape[1] + row_ids
    block_at = cols_ref[...]
    used = slot_ids < count_ref[...]
    far_code = jnp.int32(1 << 30)

    def held(first_row, holder):
        inside = (row_ids >= first_row) & (row_ids < first_row + rows)
        return used & inside & (block_at >= holder * holders) & (block_at < (holder + 1) * holders)

    def wanted(dest):
        mine = held(dest * rows, me)
        code = block_ids * BLK + (block_at - me * holders)
        low_code = jnp.min(jnp.where(mine, code, far_code))
        high_code = jnp.max(jnp.where(mine, code, 0))
        return (low_code & (BLK - 1), high_code & (BLK - 1))

    def send_cols(j):
        dest = lax.rem(me + j, n)
        for q, at in enumerate(wanted(dest)):
            colsend[dest * CAP + q] = cotb[at]
        cols(j).start()

    def pair_copy(zd, c):
        return remote(ysend.at[zd, c], yrecv.at[zd, c], ys_sem.at[zd, c], yr_sem.at[zd, c], mp=pair)

    def product(slot, c):
        return lax.dot_general(
            cot_ref[...], wbuf[slot, pl.ds(pl.multiple_of(c * PIECE, PIECE), PIECE), :],
            contract_last, preferred_element_type=jnp.float32,
        ).astype(jnp.bfloat16)

    def refill(i):
        @pl.when(i + 2 < 2 * outer)
        def _():
            fetch(i + 2).start()

    def edge(zd, c):
        return ((zd == 0) | (zd == outer - 1)) & (c == pieces - 1)

    def chain_first(zd, c):
        return edge(zd, c) & (zd != z)

    def far_item(i):
        zd, _ = item_owner(i)
        slot = lax.rem(i, 2)
        fetch(i).wait()

        def one(c):
            ysend[zd, c] = product(slot, c)

            @pl.when(jnp.logical_not(edge(zd, c)))
            def _():
                pair_copy(zd, c).start()

        loop(pieces, one)
        refill(i)

    def near_item(i):
        zd, _ = item_owner(i)
        slot = lax.rem(i, 2)
        fetch(i).wait()

        def one(c):
            own[zd, c] = product(slot, c)

        loop(pieces, one)
        refill(i)

    far_item(jnp.int32(0))
    loop(n, send_cols, 1)
    for q, at in enumerate(wanted(me)):
        colgot[me * CAP + q] = cotb[at]
    colgot[n * CAP] = jnp.zeros((tok, BLK), jnp.bfloat16)
    loop(outer, far_item, 1)

    loop(n, lambda j: lb1_in(j).wait_recv(), 1)
    lbgot[me] = lbpart[me]
    total = lbgot[0].astype(jnp.float32)
    for i in range(1, n):
        total = total + lbgot[i].astype(jnp.float32)
    lbfull[me] = total.astype(jnp.bfloat16)
    loop(n, lambda j: lb2(j).start(), 1)

    loop(2 * outer, near_item, outer)

    def up_copy(zd, c):
        return remote(own.at[zd, c], zrecv.at[zd, c], zs_sem.at[zd, c], zr_sem.at[zd, c], mp=me + INNER)

    def down_copy(zd, c):
        slot = jnp.where(zd == z - 1, outer, zd)
        return remote(own.at[zd, c], zrecv.at[slot, c], zs_sem.at[zd, c], zr_sem.at[slot, c], mp=me - INNER)

    def chain_in(slot, c):
        return remote(own.at[0, c], zrecv.at[slot, c], zs_sem.at[0, c], zr_sem.at[slot, c], mp=pair)

    def cross(slot):
        zd = slot * (outer - 1)
        ahead = jnp.where(zd > z, me + INNER, me - INNER)
        return remote(
            ysend.at[zd, pieces - 1], crossrecv.at[slot], xs_sem.at[slot], xr_sem.at[slot], mp=ahead
        )

    def cross_in(slot):
        return remote(
            ysend.at[0, 0], crossrecv.at[slot], xs_sem.at[slot], xr_sem.at[slot], mp=pair
        )

    def cross_add(slot, zd):
        cross_in(slot).wait_recv()
        ysend[zd, pieces - 1] = (
            ysend[zd, pieces - 1].astype(jnp.float32) + crossrecv[slot].astype(jnp.float32)
        ).astype(jnp.bfloat16)

    def forward(s):
        zd = pick(s)
        incoming = ((zd > z) & (z > 0)) | ((zd < z) & (z < outer - 1))

        def one(c):
            direct = chain_first(zd, c)
            slot = jnp.where(zd == 0, 0, 1)

            @pl.when(direct)
            def _():
                @pl.when(incoming)
                def _():
                    cross_add(slot, zd)
                    chain_in(zd, c).wait_recv()
                    own[zd, c] = (
                        own[zd, c].astype(jnp.float32) + zrecv[zd, c].astype(jnp.float32)
                    ).astype(jnp.bfloat16)

                cross(slot).start()

            @pl.when(jnp.logical_not(direct))
            def _():
                pair_copy(zd, c).wait_recv()

                @pl.when(incoming)
                def _():
                    chain_in(zd, c).wait_recv()
                    own[zd, c] = (
                        own[zd, c].astype(jnp.float32)
                        + yrecv[zd, c].astype(jnp.float32)
                        + zrecv[zd, c].astype(jnp.float32)
                    ).astype(jnp.bfloat16)

                @pl.when(jnp.logical_not(incoming))
                def _():
                    own[zd, c] = (
                        own[zd, c].astype(jnp.float32) + yrecv[zd, c].astype(jnp.float32)
                    ).astype(jnp.bfloat16)

            @pl.when(zd > z)
            def _():
                up_copy(zd, c).start()

            @pl.when(zd < z)
            def _():
                down_copy(zd, c).start()

        loop(pieces, one)

    loop(outer - 1, forward)

    @pl.when(edge(z, pieces - 1))
    def _():
        cross_add(jnp.where(z == 0, 0, 1), z)
        pair_copy(z, pieces - 1).start()

    index_ref[...] = jnp.full(shape, n * CAP, jnp.int32)

    def place(holder):
        mine = held(me * rows, holder)
        first = jnp.min(jnp.where(mine, block_ids, far_code))
        rank = jnp.where(block_ids > first, 1, 0)
        index_ref[...] = jnp.where(mine, holder * CAP + rank, index_ref[...])

    loop(n, place)

    loop(n, lambda j: lb2_in(j).wait_recv(), 1)
    both = lbfull[...].reshape(tok, 128)
    low16 = both[:, 0:64]
    back16 = (adapter_scale * both[:, 64:128].astype(jnp.float32)).astype(jnp.bfloat16)

    def dcopy():
        return remote(dsend, drecv, dps.at[0], dpr.at[0], dp=1 - core)

    def ucopy():
        return remote(usend, urecv, dps.at[1], dpr.at[1], dp=1 - core)

    def bcopy(a):
        return remote(bgsend.at[a], bgrecv.at[a], dps.at[2 + a], dpr.at[2 + a], dp=1 - core)

    dsend[...] = (
        loss_scale
        * lax.dot_general(back16, act_ref[...], contract_first, preferred_element_type=jnp.float32)
    ).astype(jnp.bfloat16)
    dcopy().start()
    usend[...] = (
        loss_scale
        * adapter_scale
        * lax.dot_general(low16, cot_ref[...], contract_first, preferred_element_type=jnp.float32)
    ).astype(jnp.bfloat16)
    ucopy().start()

    values_in.wait()
    loop(n, lambda j: cols_in(j).wait_recv(), 1)
    half = MAXR * BLK // 2

    def block_row(a):
        for k in range(MAXR):
            lanes = slice(k * BLK, (k + 1) * BLK)
            here = (slot_ids == k) & (row_ids == me * rows + a)
            cat[:, lanes] = colgot[jnp.sum(jnp.where(here, index_ref[...], 0))]
            vcat[:, k * BLK:(k + 1) * BLK] = values_ref[a, k]
        first = pl.multiple_of(a * BLK, BLK)
        act_row = act_ref[:, pl.ds(first, BLK)]
        bgtmp[...] = loss_scale * lax.dot_general(
            act_row, cat[...], contract_first, preferred_element_type=jnp.float32
        )
        bgkeep[a] = bgtmp[:, pl.ds(pl.multiple_of(core * half, half), half)]
        bgsend[a] = bgtmp[:, pl.ds(pl.multiple_of((1 - core) * half, half), half)].astype(jnp.bfloat16)
        bcopy(a).start()
        sparse[:, pl.ds(first, BLK)] = lax.dot_general(
            cat[...], vcat[...], contract_last, preferred_element_type=jnp.float32
        ) + jnp.dot(back16, down_ref[:, pl.ds(first, BLK)], preferred_element_type=jnp.float32)

    loop(rows, block_row)

    dcopy().wait_recv()
    ucopy().wait_recv()
    down_out[...] = dsend[...].astype(jnp.float32) + drecv[...].astype(jnp.float32)
    up_out[...] = usend[...].astype(jnp.float32) + urecv[...].astype(jnp.float32)

    def block_sum(a):
        bcopy(a).wait_recv()
        for k in range(MAXR // 2):
            lanes = slice(k * BLK, (k + 1) * BLK)
            blocks_out[a, k] = bgkeep[a, :, lanes] + bgrecv[a, :, lanes].astype(jnp.float32)

    loop(rows, block_sum)

    def last(c):
        lanes = pl.ds(pl.multiple_of(c * PIECE, PIECE), PIECE)
        pair_copy(z, c).wait_recv()
        sparse[:, lanes] += own[z, c].astype(jnp.float32) + yrecv[z, c].astype(jnp.float32)

        @pl.when(z > 0)
        def _():
            chain_in(z, c).wait_recv()
            sparse[:, lanes] += zrecv[z, c].astype(jnp.float32)

        @pl.when(z < outer - 1)
        def _():
            chain_in(outer, c).wait_recv()
            sparse[:, lanes] += zrecv[outer, c].astype(jnp.float32)

        out_ref[:, lanes] = sparse[:, lanes].astype(jnp.bfloat16)

    loop(pieces, last)

    def drain(s):
        def one(c):
            @pl.when(jnp.logical_not(chain_first(s, c)))
            def _():
                pair_copy(s, c).wait_send()

            @pl.when(chain_first(s, c))
            def _():
                cross(jnp.where(s == 0, 0, 1)).wait_send()

            @pl.when(s > z)
            def _():
                up_copy(s, c).wait_send()

            @pl.when(s < z)
            def _():
                down_copy(s, c).wait_send()

        loop(pieces, one)

    loop(outer, drain)

    def drain_small(j):
        lb1(j).wait_send()
        lb2(j).wait_send()
        cols(j).wait_send()

    loop(n, drain_small, 1)
    dcopy().wait_send()
    ucopy().wait_send()
    loop(rows, lambda a: bcopy(a).wait_send())


def local(
    activations,
    cotangent,
    frozen_weight,
    adapter_down,
    adapter_up,
    sparse_values,
    block_cols,
    block_count,
):
    tok, wide = activations.shape
    hidden = cotangent.shape[1]
    n = lax.axis_size("mp")
    per_owner = wide // BLK
    per_holder = hidden // BLK
    outer = n // INNER
    pieces = wide // PIECE
    part = tok // n
    bf, f32 = jnp.bfloat16, jnp.float32
    half = MAXR * BLK // 2
    vmem = pl.BlockSpec(memory_space=pltpu.VMEM)
    anywhere = pl.BlockSpec(memory_space=pl.ANY)
    dma = pltpu.SemaphoreType.DMA
    input_grad, down_turned, up_grad, block_grads = pl.pallas_call(
        functools.partial(kernel, n),
        out_shape=(
            jax.ShapeDtypeStruct((tok, wide), bf),
            jax.ShapeDtypeStruct((64, wide), f32),
            jax.ShapeDtypeStruct((64, hidden), f32),
            jax.ShapeDtypeStruct((per_owner, MAXR // 2, BLK, BLK), f32),
        ),
        in_specs=[vmem, vmem, vmem, vmem, anywhere, vmem, vmem, anywhere],
        out_specs=(vmem, vmem, vmem, vmem),
        scratch_shapes=[
            pltpu.VMEM(sparse_values.shape, bf),
            pltpu.VMEM(block_cols.shape[::-1], jnp.int32),
            pltpu.VMEM((2, wide, hidden), bf),
            pltpu.VMEM((outer, pieces, tok, PIECE), bf),
            pltpu.VMEM((outer, pieces, tok, PIECE), bf),
            pltpu.VMEM((outer, pieces, tok, PIECE), bf),
            pltpu.VMEM((outer + 1, pieces, tok, PIECE), bf),
            pltpu.VMEM((2, tok, PIECE), bf),
            pltpu.VMEM((per_holder, tok, BLK), bf),
            pltpu.VMEM((n * CAP, tok, BLK), bf),
            pltpu.VMEM((n * CAP + 1, tok, BLK), bf),
            pltpu.VMEM((tok, MAXR * BLK), bf),
            pltpu.VMEM((BLK, MAXR * BLK), bf),
            pltpu.VMEM((tok, wide), f32),
            pltpu.VMEM((BLK, MAXR * BLK), f32),
            pltpu.VMEM((per_owner, BLK, half), f32),
            pltpu.VMEM((per_owner, BLK, half), bf),
            pltpu.VMEM((per_owner, BLK, half), bf),
            pltpu.VMEM((n, part, 128), bf),
            pltpu.VMEM((n, part, 128), bf),
            pltpu.VMEM((n, part, 128), bf),
            pltpu.VMEM((64, wide), bf),
            pltpu.VMEM((64, wide), bf),
            pltpu.VMEM((64, hidden), bf),
            pltpu.VMEM((64, hidden), bf),
            dma((1,)),
            dma((2,)),
            dma((outer, pieces)),
            dma((outer, pieces)),
            dma((outer, pieces)),
            dma((outer + 1, pieces)),
            dma((2,)),
            dma((2,)),
            dma((n,)),
            dma((n,)),
            dma((n,)),
            dma((n,)),
            dma((n,)),
            dma((n,)),
            dma((2 + per_owner,)),
            dma((2 + per_owner,)),
        ],
        compiler_params=pltpu.CompilerParams(
            collective_id=0, has_side_effects=True, vmem_limit_bytes=60 * 1024 * 1024
        ),
    )(
        block_cols.T,
        block_count.reshape(1, -1),
        activations,
        cotangent,
        frozen_weight,
        adapter_down.T,
        adapter_up,
        sparse_values,
    )
    return input_grad, down_turned.T, up_grad, block_grads


def solution(mesh):
    return jax.shard_map(
        local,
        mesh=mesh,
        in_specs=(
            P(("groups", "dp"), "mp"),
            P(("groups", "dp"), "mp"),
            P(None, "mp"),
            P("mp", None),
            P(None, "mp"),
            P("mp", None, None, None),
            P(),
            P(),
        ),
        out_specs=(
            P(("groups", "dp"), "mp"),
            P(("groups", "mp"), None),
            P("groups", "mp"),
            P(("groups", "mp"), "dp", None, None),
        ),
        check_vma=False,
    )
```
